128 devices in a mesh: tok: 8 (over z_lo, y), vocab: 16 (over z_hi, x, core).
Axes of the slice: x: 4, y: 4, z: 4 (z_hi: 2, z_lo: 2; z = z_hi * 2 + z_lo), core: 2. Of those that a mesh axis runs over, the one named last changes fastest.
Arguments:
- hidden_rows: bfloat16 [1024, 24576], P(('tok', 'vocab')), may hold values from -6 to 6
- join_weight: bfloat16 [24576, 8192], P('vocab', 'tok'), may hold values from -0.0390625 to 0.0390625
- norm_gain: float32 [8192], P('tok'), may hold values from 0.2 to 4.5
- head_weight: bfloat16 [8192, 65536], P('tok', 'vocab'), may hold values from -26 to 26
- targets: int32 [1024], replicated, may hold values from 0 to 65535
Outputs:
- token_loss: float32 [1024], P('tok')
- gain_grad: float32 [8192], P('tok')
- join_grad: bfloat16 [24576, 8192], P('vocab', 'tok')
The draws below stay inside these ranges and needn't reach their ends.
All inputs are finite; a program needn't handle non-finite values.
Results may differ from the reference program's by a relative error of at most 0.02.
The reference program's roundings to bfloat16 on the way (of `normed`, `logit_grad` and `dfused`) count: a program that leaves them out, or rounds other values in their place, can miss the bound.
Values may be sent and summed in bfloat16 or wider, within the bound.
No kernel may reach another device: no remote copies, remote signals or barrier semaphores. Data moves between devices by JAX's collectives and lax.ppermute only.
A program may use at most 128 MiB of HBM per device.

```python
import math
import jax
import jax.numpy as jnp
from jax import lax

D = 8192
VOCAB = 65536
TOKENS = 1024


def draw_head_weight(key, part):
    key = jax.random.fold_in(key, 11)
    first_key = jax.random.fold_in(key, 0)
    third_key = jax.random.fold_in(key, 2)
    column_scale = jax.random.uniform(third_key, (1, VOCAB), jnp.float32, 0.7, 1.3)
    values = jnp.clip(jax.random.normal(first_key, (D, VOCAB), jnp.float32), -6.0, 6.0)
    return (values * column_scale * 3.0 / math.sqrt(D)).astype(jnp.bfloat16)


def draw_norm_gain(key, part):
    key = jax.random.fold_in(key, 23)
    position = jnp.arange(D, dtype=jnp.float32) / (D - 1)
    factor = jax.random.uniform(key, (D,), jnp.float32, 0.6, 1.4)
    return 0.5 * jnp.exp(math.log(4.0) * position) * factor


def plant(result, rng, low, largest):
    longest = result.shape.index(max(result.shape))
    spots = []
    for shift in (0, 1):
        where = [jax.random.randint(jax.random.fold_in(rng, axis), (), 0, length) for axis, length in enumerate(result.shape)]
        where[longest] = (where[longest] + shift) % result.shape[longest]
        spots.append(tuple(where))
    return result.at[spots[0]].set(low).at[spots[1]].set(largest)


def shard_levels(rng, dims, cuts, smallest, top_value):
    def one(axis_at, blocks):
        draws = jax.random.uniform(jax.random.fold_in(jax.random.fold_in(rng, 6), axis_at), (blocks,), jnp.float32, smallest / len(cuts), top_value / len(cuts))
        return jnp.repeat(jnp.exp(draws), dims[axis_at] // blocks).reshape((-1,) + (1,) * (len(dims) - axis_at - 1))

    loudness = one(*cuts[0])
    for cut in cuts[1:]:
        loudness = loudness * one(*cut)
    return loudness


def gaussian(stream_key, extent, deviation, bound, shards=(), kind=jnp.bfloat16):
    array = deviation * jax.random.normal(stream_key, extent, jnp.float32)
    if shards:
        array = array * shard_levels(stream_key, extent, shards, -0.22, 0.18)
    return jnp.clip(array, -bound, bound).astype(kind)


def setup_inputs(seed: int = 0) -> dict:
    streams_of = jax.random.split(jax.random.key(seed), 6)
    hidden_rows = gaussian(streams_of[0], (TOKENS, 3 * D), 1.0, 6.0, ((0, 128),))
    join_weight = gaussian(streams_of[1], (3 * D, D), (3 * D) ** -0.5, 0.0390625, ((0, 16), (1, 8)))
    norm_gain = draw_norm_gain(jax.random.fold_in(streams_of[5], 71), 0)
    head_weight = draw_head_weight(jax.random.fold_in(streams_of[5], 71), 0)
    targets = plant(jax.random.randint(streams_of[4], (TOKENS,), 0, VOCAB), jax.random.fold_in(streams_of[4], 1), 0, VOCAB - 1).astype(jnp.int32)
    return dict(hidden_rows=hidden_rows, join_weight=join_weight, norm_gain=norm_gain, head_weight=head_weight, targets=targets)


epsilon = 1e-05

def reference(hidden_rows, join_weight, norm_gain, head_weight, targets):
    joined_rows = jnp.dot(hidden_rows, join_weight, preferred_element_type=jnp.float32)
    inverse_rms = lax.rsqrt(lax.optimization_barrier(jnp.sum(joined_rows * joined_rows, axis=1, keepdims=True)) / D + epsilon)
    unit_rows = joined_rows * inverse_rms
    normed = (unit_rows * norm_gain).astype(jnp.bfloat16)
    logits = jnp.dot(normed, head_weight, preferred_element_type=jnp.float32)
    row_top = lax.optimization_barrier(jnp.max(logits, axis=1, keepdims=True))
    row_total = lax.optimization_barrier(jnp.sum(jnp.exp(logits - row_top), axis=1, keepdims=True))
    columns = lax.broadcasted_iota(jnp.int32, logits.shape, 1)
    target_hit = columns == targets.astype(jnp.int32)[:, None]
    picked = lax.optimization_barrier(jnp.sum(jnp.where(target_hit, logits, 0.0), axis=1, keepdims=True))
    token_loss = (jnp.log(row_total) + row_top - picked)[:, 0]
    logit_grad = (jnp.exp(logits - row_top) / row_total - target_hit.astype(jnp.float32)).astype(jnp.bfloat16)
    dnormed = lax.dot_general(logit_grad, head_weight, (((1,), (1,)), ((), ())), preferred_element_type=jnp.float32)
    gain_grad = lax.optimization_barrier(jnp.sum(dnormed * unit_rows, axis=0))
    unit_grad = dnormed * norm_gain
    inner_dots = lax.optimization_barrier(jnp.sum(unit_grad * unit_rows, axis=1, keepdims=True)) / D
    dfused = (inverse_rms * (unit_grad - unit_rows * inner_dots)).astype(jnp.bfloat16)
    join_grad = lax.dot_general(hidden_rows, dfused, (((0,), (0,)), ((), ())), preferred_element_type=jnp.float32)
    return (token_loss, gain_grad, join_grad.astype(jnp.bfloat16))
```

```python
import jax
import jax.numpy as jnp
from jax import lax
from jax.sharding import PartitionSpec as P

epsilon = 1e-05
F32, F16, BF16 = jnp.float32, jnp.float16, jnp.bfloat16

AXES = {"z": ("tok", 4, 2), "y": ("tok", 1, 4), "zh": ("vocab", 8, 2), "x": ("vocab", 2, 4), "c": ("vocab", 1, 2)}
SIZE = {"tok": 8, "vocab": 16}
UP = 6


def coord(name):
    axis, stride, size = AXES[name]
    return (lax.axis_index(axis) // stride) % size


def send(value, name, shift):
    axis, stride, size = AXES[name]
    perm = []
    for i in range(SIZE[axis]):
        at = (i // stride) % size
        perm.append((i, i + ((at + shift) % size - at) * stride))
    return lax.ppermute(value, axis, perm)


def fetch(value, name, ahead):
    return send(value, name, -ahead)


def to_relative(value, dim, name):
    size = AXES[name][2]
    return lax.dynamic_slice_in_dim(jnp.concatenate([value, value], dim), coord(name), size, dim)


def to_absolute(value, dim, name):
    size = AXES[name][2]
    return lax.dynamic_slice_in_dim(jnp.concatenate([value, value], dim), size - coord(name), size, dim)


def pack(value, scale):
    return (value * scale).astype(F16)


def unpack(value, scale):
    return value.astype(F32) * (1.0 / scale)


def sum_slots(value, name, scale):
    total = value[0]
    for d in range(1, AXES[name][2]):
        total = total + unpack(send(pack(value[d], scale), name, d), scale)
    return total


def gather_slots(value, name):
    return jnp.stack([value] + [fetch(value, name, d) for d in range(1, AXES[name][2])])


def sum_vocab(left, weight, dims, scale):
    _, nx, nh, rows, depth = left.shape

    def product(part):
        return lax.dot_general(part.reshape(-1, depth), weight, dims, preferred_element_type=F32)

    theirs = send(pack(product(left[1]), scale), "c", 1)
    ours = product(left[0]) + unpack(theirs, scale)
    ours = sum_slots(ours.reshape(nx, nh, rows, -1), "x", scale)
    return sum_slots(ours, "zh", scale)


def gather_vocab(value):
    return gather_slots(gather_slots(gather_slots(value, "zh"), "x"), "c")


def sum_tok_rows(value):
    total = value
    for d in range(1, 4):
        total = total + jnp.roll(fetch(value, "y", d), d, 1)
    return total + jnp.roll(fetch(total, "z", 1), 1, 0)


def sum_vocab_all(value):
    for name in ("c", "x", "zh"):
        total = value
        for d in range(1, AXES[name][2]):
            total = total + fetch(value, name, d)
        value = total
    return value


def gather_tok(value, up):
    other = fetch(value, "z", 1)
    late = value[up:]
    late_y = [fetch(late, "y", d) for d in range(1, 4)]
    early = jnp.stack([value[:up], other[:up]])
    early = [early] + [fetch(early, "y", d) for d in range(1, 4)]
    far = [other[up:]] + [fetch(part, "z", 1) for part in late_y]
    late = [jnp.stack([near, there]) for near, there in zip([late] + late_y, far)]
    return tuple(jnp.stack(part, 1).transpose(2, 0, 1, 3, 4) for part in (early, late))


def sum_tok(left_up, left_late, weight, scale):
    def product(part):
        return lax.dot_general(
            part.reshape(-1, part.shape[-1]), weight, (((1,), (0,)), ((), ())), preferred_element_type=F32
        )

    rep = left_up.shape[3]
    late = left_late.transpose(1, 2, 0, 3, 4)
    up = left_up.transpose(2, 1, 0, 3, 4)
    there = send(pack(product(late[1]), scale), "z", 1)
    sent = [send(pack(product(up[d]), scale), "y", d) for d in range(1, 4)]
    up_sum = product(up[0])
    for part in sent:
        up_sum = up_sum + unpack(part, scale)
    up_sum = sum_slots(up_sum.reshape(2, -1, up_sum.shape[-1]), "z", scale)
    late_sum = product(late[0]) + unpack(there, scale)
    late_sum = sum_slots(late_sum.reshape(4, -1, late_sum.shape[-1]), "y", scale)
    return jnp.concatenate([up_sum, late_sum], 0)


def merge(states):
    top = states[0][0]
    for other in states[1:]:
        top = jnp.maximum(top, other[0])
    total = sum(state[1] * jnp.exp(state[0] - top) for state in states)
    picked = sum(state[2] for state in states)
    return jnp.stack([top, total, picked])


def softmax_rows(logits, wanted, first_column, rep):
    columns = first_column + lax.broadcasted_iota(jnp.int32, logits.shape, 1)
    target_hit = columns == wanted[:, None]
    picked = jnp.sum(jnp.where(target_hit, logits, 0.0), axis=1)
    top = jnp.max(logits, axis=1)
    total = jnp.sum(jnp.exp(logits - top[:, None]), axis=1)
    state = jnp.stack([top, total, picked]).reshape(3, 2, 4, 2, rep)
    for name, dim in (("c", 1), ("x", 2), ("zh", 3)):
        state = merge([state] + [jnp.roll(fetch(state, name, d), d, dim) for d in range(1, AXES[name][2])])
    row_top, row_total, picked = state.reshape(3, -1)
    token_loss = jnp.log(row_total) + row_top - picked
    probable = jnp.exp(logits - row_top[:, None]) / row_total[:, None]
    logit_grad = (probable - target_hit.astype(F32)).astype(BF16)
    return token_loss, logit_grad


def body(hidden_rows, join_weight, norm_gain, head_weight, targets):
    tok_index = lax.axis_index("tok")
    voc_index = lax.axis_index("vocab")
    width = join_weight.shape[1]
    full_width = width * 8
    rep = hidden_rows.shape[0]
    depth = join_weight.shape[0]
    own = targets.shape[0] // 8

    def relative(value):
        value = to_relative(to_relative(to_relative(value, 0, "zh"), 1, "x"), 2, "c")
        return value.transpose((2, 1, 0) + tuple(range(3, value.ndim)))

    wanted = lax.dynamic_slice_in_dim(targets, tok_index * own, own, 0)
    wanted = relative(wanted.reshape(2, 4, 2, rep)).reshape(-1)

    spread = lax.all_to_all(hidden_rows, "vocab", split_axis=1, concat_axis=0, tiled=True)
    spread = relative(spread.reshape(2, 4, 2, rep, depth)).reshape(16, rep, depth)
    inputs = jnp.concatenate(gather_tok(spread, UP), 0)

    rows = 8 * rep
    joined = sum_vocab(inputs.reshape(2, 4, 2, rows, depth), join_weight, (((1,), (0,)), ((), ())), 8.0)
    squares = sum_tok_rows(jnp.sum(joined * joined, axis=1).reshape(2, 4, rep)).reshape(-1)
    inverse_rms = lax.rsqrt(squares / full_width + epsilon)[:, None]
    unit_rows = joined * inverse_rms
    normed = gather_vocab((unit_rows * norm_gain).astype(BF16)).reshape(16, 2, 4, rep, width)
    logits = sum_tok(normed[:UP], normed[UP:], head_weight, 1.0 / 16)
    token_loss, logit_grad = softmax_rows(logits, wanted, voc_index * head_weight.shape[1], rep)
    token_loss = token_loss.reshape(2, 4, 2, rep).transpose(2, 1, 0, 3)
    token_loss = to_absolute(to_absolute(to_absolute(token_loss, 0, "zh"), 1, "x"), 2, "c").reshape(-1)

    grads = jnp.concatenate(gather_tok(logit_grad.reshape(16, rep, -1), UP), 0)
    dnormed = sum_vocab(grads.reshape(2, 4, 2, rows, -1), head_weight, (((1,), (1,)), ((), ())), 1024.0)
    gain_grad = sum_vocab_all(jnp.sum(dnormed * unit_rows, axis=0))
    unit_grad = dnormed * norm_gain
    inner = sum_tok_rows(jnp.sum(unit_grad * unit_rows, axis=1).reshape(2, 4, rep)).reshape(-1)
    dfused = (inverse_rms * (unit_grad - unit_rows * (inner / full_width)[:, None])).astype(BF16)
    dfused = gather_vocab(dfused).reshape(-1, width)
    join_grad = lax.dot_general(
        inputs.reshape(-1, depth), dfused, (((0,), (0,)), ((), ())), preferred_element_type=F32
    )
    return (token_loss, gain_grad, join_grad.astype(BF16))


def solution(mesh):
    placed = (P(("tok", "vocab"), None), P("vocab", "tok"), P("tok"), P("tok", "vocab"), P())
    return jax.shard_map(
        body,
        mesh=mesh,
        in_specs=placed,
        out_specs=(P("tok"), P("tok"), P("vocab", "tok")),
        check_vma=False,
    )
```

```python
import jax
import jax.numpy as jnp
from jax import lax
from jax.sharding import PartitionSpec as P

epsilon = 1e-05
F32, F16, BF16 = jnp.float32, jnp.float16, jnp.bfloat16

AXES = {"z": ("tok", 4, 2), "y": ("tok", 1, 4), "zh": ("vocab", 8, 2), "x": ("vocab", 2, 4), "c": ("vocab", 1, 2)}
SIZE = {"tok": 8, "vocab": 16}


def coord(name):
    axis, stride, size = AXES[name]
    return (lax.axis_index(axis) // stride) % size


def send(value, name, shift):
    axis, stride, size = AXES[name]
    perm = []
    for i in range(SIZE[axis]):
        at = (i // stride) % size
        perm.append((i, i + ((at + shift) % size - at) * stride))
    return lax.ppermute(value, axis, perm)


def fetch(value, name, ahead):
    return send(value, name, -ahead)


def to_relative(value, dim, name):
    size = AXES[name][2]
    return lax.dynamic_slice_in_dim(jnp.concatenate([value, value], dim), coord(name), size, dim)


def to_absolute(value, dim, name):
    size = AXES[name][2]
    return lax.dynamic_slice_in_dim(jnp.concatenate([value, value], dim), size - coord(name), size, dim)


def pack(value, scale):
    return (value * scale).astype(F16)


def unpack(value, scale):
    return value.astype(F32) * (1.0 / scale)


def swap_sides(mine, other, name):
    first = coord(name) == 0
    return jnp.where(first, mine, other), jnp.where(first, other, mine)


def sum_slots(value, name, scale):
    sent = [send(pack(value[d], scale), name, d) for d in range(1, AXES[name][2])]
    total = value[0]
    for part in sent:
        total = total + unpack(part, scale)
    return total


def gather_slots(value, name):
    return jnp.stack([value] + [fetch(value, name, d) for d in range(1, AXES[name][2])])


def sum_core_x(left, weight, dims, scale):
    _, nx, rows, depth = left.shape

    def product(part):
        return lax.dot_general(part.reshape(-1, depth), weight, dims, preferred_element_type=F32)

    theirs = send(pack(product(left[1]), scale), "c", 1)
    ours = product(left[0]) + unpack(theirs, scale)
    return sum_slots(ours.reshape(nx, rows, -1), "x", scale)


def sum_zh(first, second, scale):
    mine, other = swap_sides(first, second, "zh")
    return mine + unpack(send(pack(other, scale), "zh", 1), scale)


def sum_tok_rows(value):
    total = value
    for d in range(1, 4):
        total = total + jnp.roll(fetch(value, "y", d), d, 1)
    return total + jnp.roll(fetch(total, "z", 1), 1, 0)


def gather_tok(value):
    other = fetch(value, "z", 1)
    near = [value] + [fetch(value, "y", d) for d in range(1, 4)]
    far = [other] + [fetch(other, "y", d) for d in range(1, 4)]
    return jnp.stack([jnp.stack(near), jnp.stack(far)])


def merge(states):
    top = states[0][0]
    for other in states[1:]:
        top = jnp.maximum(top, other[0])
    total, moment, picked = 0.0, 0.0, 0.0
    for state in states:
        below = state[0] - top
        factor = jnp.exp(below)
        total = total + state[1] * factor
        moment = moment + (state[2] + state[1] * below) * factor
        picked = picked + state[3]
    return jnp.stack([top, total, moment, picked])


def softmax_rows(logits, wanted, first_column, rep):
    columns = first_column + lax.broadcasted_iota(jnp.int32, logits.shape, 1)
    target_hit = columns == wanted[:, None]
    picked = jnp.sum(jnp.where(target_hit, logits, 0.0), axis=1)
    top = jnp.max(logits, axis=1)
    below = logits - top[:, None]
    weights = jnp.exp(below)
    total = jnp.sum(weights, axis=1)
    moment = jnp.sum(weights * below, axis=1)
    state = jnp.stack([top, total, moment, picked]).reshape(4, 2, 2, 4, rep)
    for name, dim in (("c", 2), ("z", 1), ("x", 3), ("zh", None)):
        others = [fetch(state, name, d) for d in range(1, AXES[name][2])]
        if dim is not None:
            others = [jnp.roll(other, d + 1, dim) for d, other in enumerate(others)]
        state = merge([state] + others)
    row_top, row_total, moment, picked = state.reshape(4, -1)
    token_loss = jnp.log(row_total) + row_top - picked
    inner = moment / row_total + (row_top - picked)
    probable = jnp.exp(logits - row_top[:, None]) / row_total[:, None]
    logit_grad = (probable - target_hit.astype(F32)).astype(BF16)
    return token_loss, logit_grad, inner


def body(hidden_rows, join_weight, norm_gain, head_weight, targets):
    depth, width = join_weight.shape
    full_width = width * 8
    rep = hidden_rows.shape[0]
    rows = 8 * rep
    own = targets.shape[0] // 8
    half = head_weight.shape[1] // 2
    z, y, zh = coord("z"), coord("y"), coord("zh")

    kept = lax.dynamic_slice_in_dim(head_weight, z * half, half, 1)
    given = lax.dynamic_slice_in_dim(head_weight, (1 - z) * half, half, 1)
    head = jnp.concatenate([kept, send(given, "z", 1)], 0)
    first_column = lax.axis_index("vocab") * head_weight.shape[1] + z * half

    def relative(value):
        value = to_relative(to_relative(value, 1, "x"), 2, "c")
        return value.transpose((2, 1, 0) + tuple(range(3, value.ndim)))

    wanted = lax.dynamic_slice_in_dim(targets.reshape(2, 4, own), y, 1, 1).reshape(2, 2, 4, 2, rep)
    wanted = to_relative(wanted, 0, "z").transpose(1, 2, 3, 0, 4)
    wanted = relative(wanted).transpose(2, 3, 0, 1, 4).reshape(2, -1)

    spread = lax.all_to_all(hidden_rows, "vocab", split_axis=1, concat_axis=0, tiled=True)
    spread = relative(spread.reshape(2, 4, 2, rep, depth))
    inputs = gather_tok(spread).transpose(2, 3, 4, 0, 1, 5, 6)

    joined = sum_core_x(inputs.reshape(2, 4, 2 * rows, depth), join_weight, (((1,), (0,)), ((), ())), 8.0)
    joined = sum_zh(joined[:rows], joined[rows:], 8.0)
    squares = sum_tok_rows(jnp.sum(joined * joined, axis=1).reshape(2, 4, rep)).reshape(-1)
    inverse_rms = lax.rsqrt(squares / full_width + epsilon)[:, None]
    unit_rows = joined * inverse_rms
    normed = (unit_rows * norm_gain).astype(BF16)

    def flip_z(value):
        return jnp.roll(value.reshape(2, 4 * rep, -1), 1, 0).reshape(value.shape)

    normed = jnp.concatenate([normed, flip_z(fetch(normed, "z", 1))], 1)
    chunks = swap_sides(normed, fetch(normed, "zh", 1), "zh")

    losses, inners, sums = [], [], []
    for k in range(2):
        normed = gather_slots(gather_slots(chunks[k], "x"), "c").reshape(2, 4, 2, 4, rep, -1)
        normed = normed.transpose(3, 2, 0, 1, 4, 5).reshape(4, -1, normed.shape[-1])
        there = jnp.dot(normed[1:].reshape(-1, normed.shape[-1]), head, preferred_element_type=F32)
        there = pack(there, 1.0 / 16).reshape(3, -1, half)
        sent = [send(there[d - 1], "y", d) for d in range(1, 4)]
        logits = jnp.dot(normed[0], head, preferred_element_type=F32)
        for part in sent:
            logits = logits + unpack(part, 1.0 / 16)
        token_loss, logit_grad, inner = softmax_rows(logits, wanted[k], first_column, rep)
        losses.append(token_loss.reshape(2, 2, 4, rep)[0])
        inners.append(inner.reshape(2, 2, 4, rep)[:, 0, 0])
        grads = gather_slots(logit_grad, "y").reshape(4, 2, 2, 4, rep, half)
        grads = grads.transpose(2, 3, 1, 0, 4, 5).reshape(2, 4, rows, half)
        sums.append(sum_core_x(grads, head, (((1,), (1,)), ((), ())), 1024.0))

    token_loss = jnp.stack(losses).transpose(0, 2, 1, 3)
    token_loss = to_absolute(to_absolute(token_loss, 1, "x"), 2, "c").reshape(-1)
    inner = jnp.where(zh == 0, inners[0], inners[1])
    inner = jnp.stack([inner] + [fetch(inner, "y", d) for d in range(1, 4)], 1).reshape(-1, 1)

    dnormed = sum_zh(sums[0], sums[1], 1024.0)
    theirs = unpack(send(pack(dnormed[:, width:], 1024.0), "z", 1), 1024.0)
    dnormed = dnormed[:, :width] + flip_z(theirs)
    unit_grad = dnormed * norm_gain
    dfused = (inverse_rms * (unit_grad - unit_rows * (inner / full_width))).astype(BF16)

    gain = jnp.sum(dnormed * unit_rows, axis=0)
    pieces = []
    for _ in range(3):
        piece = lax.reduce_precision(gain, 8, 7)
        gain = gain - piece
        pieces.append(piece.astype(BF16))
    extra = jnp.stack(pieces + [jnp.zeros_like(pieces[0])] * 5)
    message = jnp.concatenate([dfused, extra], 0)
    message = jnp.stack(swap_sides(message, fetch(message, "zh", 1), "zh"))
    message = gather_slots(gather_slots(message, "x"), "c")
    gain_grad = jnp.sum(message[:, :, :, rows : rows + 3].astype(F32), axis=(0, 1, 2, 3))
    join_grad = lax.dot_general(
        inputs.reshape(-1, depth),
        message[:, :, :, :rows].reshape(-1, width),
        (((0,), (0,)), ((), ())),
        preferred_element_type=F32,
    )
    return (token_loss, gain_grad, join_grad.astype(BF16))


def solution(mesh):
    placed = (P(("tok", "vocab"), None), P("vocab", "tok"), P("tok"), P("tok", "vocab"), P())
    return jax.shard_map(
        body,
        mesh=mesh,
        in_specs=placed,
        out_specs=(P("tok"), P("tok"), P("vocab", "tok")),
        check_vma=False,
    )
```

```python
import jax
import jax.numpy as jnp
from jax import lax
from jax.sharding import PartitionSpec as P

epsilon = 1e-05
F32, F16, BF16 = jnp.float32, jnp.float16, jnp.bfloat16

AXES = {"z": ("tok", 4, 2), "y": ("tok", 1, 4), "zh": ("vocab", 8, 2), "x": ("vocab", 2, 4), "c": ("vocab", 1, 2)}
SIZE = {"tok": 8, "vocab": 16}


def coord(name):
    axis, stride, size = AXES[name]
    return (lax.axis_index(axis) // stride) % size


def send(value, name, shift):
    axis, stride, size = AXES[name]
    perm = []
    for i in range(SIZE[axis]):
        at = (i // stride) % size
        perm.append((i, i + ((at + shift) % size - at) * stride))
    return lax.ppermute(value, axis, perm)


def fetch(value, name, ahead):
    return send(value, name, -ahead)


def to_relative(value, dim, name):
    size = AXES[name][2]
    return lax.dynamic_slice_in_dim(jnp.concatenate([value, value], dim), coord(name), size, dim)


def to_absolute(value, dim, name):
    size = AXES[name][2]
    return lax.dynamic_slice_in_dim(jnp.concatenate([value, value], dim), size - coord(name), size, dim)


def pack(value, scale):
    return (value * scale).astype(F16)


def unpack(value, scale):
    return value.astype(F32) * (1.0 / scale)


def sum_slots(value, name, scale):
    sent = [send(pack(value[d], scale), name, d) for d in range(1, AXES[name][2])]
    total = value[0]
    for part in sent:
        total = total + unpack(part, scale)
    return total


def gather_slots(value, name):
    return jnp.stack([value] + [fetch(value, name, d) for d in range(1, AXES[name][2])])


def sum_vocab(near, far, weight, dims, scale):
    nx, nh, rows, depth = near.shape

    def product(part):
        return lax.dot_general(part.reshape(-1, depth), weight, dims, preferred_element_type=F32)

    theirs = send(pack(product(far), scale), "c", 1)
    ours = product(near) + unpack(theirs, scale)
    ours = sum_slots(ours.reshape(nx, nh, rows, -1), "x", scale)
    return sum_slots(ours, "zh", scale)


def gather_x_zh(value):
    return gather_slots(gather_slots(value, "zh"), "x")


def sum_tok_rows(value):
    total = value
    for d in range(1, 4):
        total = total + jnp.roll(fetch(value, "y", d), d, 1)
    return total + jnp.roll(fetch(total, "z", 1), 1, 0)


def gather_tok(value):
    other = fetch(value, "z", 1)
    late = value[1]
    late_y = [fetch(late, "y", d) for d in range(1, 4)]
    early = jnp.stack([value[0], other[0]])
    early = [early] + [fetch(early, "y", d) for d in range(1, 4)]
    far = [other[1]] + [fetch(part, "z", 1) for part in late_y]
    late = [jnp.stack([near, there]) for near, there in zip([late] + late_y, far)]
    return tuple(jnp.stack(part, 1).transpose(2, 3, 0, 1, 4, 5) for part in (early, late))


def sum_tok(near, far, weight, scale):
    def product(part):
        return lax.dot_general(
            part.reshape(-1, part.shape[-1]), weight, (((1,), (0,)), ((), ())), preferred_element_type=F32
        )

    near = near.transpose(3, 2, 0, 1, 4, 5)
    far = far.transpose(2, 3, 0, 1, 4, 5)
    there = send(pack(product(far[1]), scale), "z", 1)
    sent = [send(pack(product(near[d]), scale), "y", d) for d in range(1, 4)]
    near_sum = product(near[0])
    for part in sent:
        near_sum = near_sum + unpack(part, scale)
    near_sum = sum_slots(near_sum.reshape(2, -1, near_sum.shape[-1]), "z", scale)
    far_sum = product(far[0]) + unpack(there, scale)
    far_sum = sum_slots(far_sum.reshape(4, -1, far_sum.shape[-1]), "y", scale)
    return jnp.concatenate([near_sum, far_sum], 0)


def merge(states):
    top = states[0][0]
    for other in states[1:]:
        top = jnp.maximum(top, other[0])
    total, moment, picked = 0.0, 0.0, 0.0
    for state in states:
        below = state[0] - top
        factor = jnp.exp(below)
        total = total + state[1] * factor
        moment = moment + (state[2] + state[1] * below) * factor
        picked = picked + state[3]
    return jnp.stack([top, total, moment, picked])


def softmax_rows(logits, wanted, first_column, rep):
    columns = first_column + lax.broadcasted_iota(jnp.int32, logits.shape, 1)
    target_hit = columns == wanted[:, None]
    picked = jnp.sum(jnp.where(target_hit, logits, 0.0), axis=1)
    top = jnp.max(logits, axis=1)
    below = logits - top[:, None]
    weights = jnp.exp(below)
    total = jnp.sum(weights, axis=1)
    moment = jnp.sum(weights * below, axis=1)
    state = jnp.stack([top, total, moment, picked]).reshape(4, 2, 4, 2, rep)
    for name, dim in (("c", 1), ("x", 2), ("zh", 3)):
        state = merge([state] + [jnp.roll(fetch(state, name, d), d, dim) for d in range(1, AXES[name][2])])
    row_top, row_total, moment, picked = state.reshape(4, -1)
    token_loss = jnp.log(row_total) + row_top - picked
    inner = moment / row_total + (row_top - picked)
    probable = jnp.exp(logits - row_top[:, None]) / row_total[:, None]
    logit_grad = (probable - target_hit.astype(F32)).astype(BF16)
    return token_loss, logit_grad, inner


def body(hidden_rows, join_weight, norm_gain, head_weight, targets):
    tok_index = lax.axis_index("tok")
    voc_index = lax.axis_index("vocab")
    width = join_weight.shape[1]
    full_width = width * 8
    rep = hidden_rows.shape[0]
    depth = join_weight.shape[0]
    own = targets.shape[0] // 8

    def relative(value):
        value = to_relative(to_relative(to_relative(value, 0, "zh"), 1, "x"), 2, "c")
        return value.transpose((2, 1, 0) + tuple(range(3, value.ndim)))

    wanted = lax.dynamic_slice_in_dim(targets, tok_index * own, own, 0)
    wanted = relative(wanted.reshape(2, 4, 2, rep)).reshape(-1)

    spread = lax.all_to_all(hidden_rows, "vocab", split_axis=1, concat_axis=0, tiled=True)
    spread = relative(spread.reshape(2, 4, 2, rep, depth))
    rows = 8 * rep
    inputs = [part.reshape(4, 2, rows, depth) for part in gather_tok(spread)]

    joined = sum_vocab(inputs[0], inputs[1], join_weight, (((1,), (0,)), ((), ())), 8.0)
    squares = sum_tok_rows(jnp.sum(joined * joined, axis=1).reshape(2, 4, rep)).reshape(-1)
    inverse_rms = lax.rsqrt(squares / full_width + epsilon)[:, None]
    unit_rows = joined * inverse_rms
    near = gather_x_zh((unit_rows * norm_gain).astype(BF16))
    far = fetch(near, "c", 1)
    near, far = (part.reshape(4, 2, 2, 4, rep, width) for part in (near, far))
    logits = sum_tok(near, far, head_weight, 1.0 / 16)
    token_loss, logit_grad, inner = softmax_rows(logits, wanted, voc_index * head_weight.shape[1], rep)
    token_loss = token_loss.reshape(2, 4, 2, rep).transpose(2, 1, 0, 3)
    token_loss = to_absolute(to_absolute(to_absolute(token_loss, 0, "zh"), 1, "x"), 2, "c").reshape(-1)
    inner = gather_slots(gather_slots(inner[:rep], "y"), "z").reshape(-1, 1)

    grads = [part.reshape(4, 2, rows, -1) for part in gather_tok(logit_grad.reshape(2, 4, 2, rep, -1))]
    dnormed = sum_vocab(grads[0], grads[1], head_weight, (((1,), (1,)), ((), ())), 1024.0)
    unit_grad = dnormed * norm_gain
    dfused = (inverse_rms * (unit_grad - unit_rows * (inner / full_width))).astype(BF16)

    gain = jnp.sum(dnormed * unit_rows, axis=0)
    pieces = []
    for _ in range(3):
        piece = lax.reduce_precision(gain, 8, 7)
        gain = gain - piece
        pieces.append(piece.astype(BF16))
    extra = jnp.stack(pieces + [jnp.zeros_like(pieces[0])] * 5)
    message = gather_x_zh(jnp.concatenate([dfused, extra], 0))
    message = jnp.stack([message, fetch(message, "c", 1)])
    gain_grad = jnp.sum(message[:, :, :, rows : rows + 3].astype(F32), axis=(0, 1, 2, 3))
    join_grad = lax.dot_general(
        jnp.stack(inputs).reshape(-1, depth),
        message[:, :, :, :rows].reshape(-1, width),
        (((0,), (0,)), ((), ())),
        preferred_element_type=F32,
    )
    return (token_loss, gain_grad, join_grad.astype(BF16))


def solution(mesh):
    placed = (P(("tok", "vocab"), None), P("vocab", "tok"), P("tok"), P("tok", "vocab"), P())
    return jax.shard_map(
        body,
        mesh=mesh,
        in_specs=placed,
        out_specs=(P("tok"), P("tok"), P("vocab", "tok")),
        check_vma=False,
    )
```

```python
import jax
import jax.numpy as jnp
from jax import lax
from jax.sharding import PartitionSpec as P

epsilon = 1e-05
F32, F16, BF16 = jnp.float32, jnp.float16, jnp.bfloat16

AXES = {"z": ("tok", 4, 2), "y": ("tok", 1, 4), "zh": ("vocab", 8, 2), "x": ("vocab", 2, 4), "c": ("vocab", 1, 2)}
SIZE = {"tok": 8, "vocab": 16}


def coord(name):
    axis, stride, size = AXES[name]
    return (lax.axis_index(axis) // stride) % size


def send(value, name, shift):
    axis, stride, size = AXES[name]
    perm = []
    for i in range(SIZE[axis]):
        at = (i // stride) % size
        perm.append((i, i + ((at + shift) % size - at) * stride))
    return lax.ppermute(value, axis, perm)


def fetch(value, name, ahead):
    return send(value, name, -ahead)


def to_relative(value, dim, name):
    size = AXES[name][2]
    return lax.dynamic_slice_in_dim(jnp.concatenate([value, value], dim), coord(name), size, dim)


def to_absolute(value, dim, name):
    size = AXES[name][2]
    return lax.dynamic_slice_in_dim(jnp.concatenate([value, value], dim), size - coord(name), size, dim)


def pack(value, scale):
    return (value * scale).astype(F16)


def unpack(value, scale):
    return value.astype(F32) * (1.0 / scale)


def sum_slots(value, name, scale):
    sent = [send(pack(value[d], scale), name, d) for d in range(1, AXES[name][2])]
    total = value[0]
    for part in sent:
        total = total + unpack(part, scale)
    return total


def gather_slots(value, name):
    return jnp.stack([value] + [fetch(value, name, d) for d in range(1, AXES[name][2])])


def sum_vocab(near, far, weight, dims, scale):
    nx, nh, rows, depth = near.shape

    def product(part):
        return lax.dot_general(part.reshape(-1, depth), weight, dims, preferred_element_type=F32)

    theirs = send(pack(product(far), scale), "c", 1)
    ours = product(near) + unpack(theirs, scale)
    ours = sum_slots(ours.reshape(nx, nh, rows, -1), "x", scale)
    return sum_slots(ours, "zh", scale)


def gather_x_zh(value):
    return gather_slots(gather_slots(value, "zh"), "x")


def ring_slots(value, name):
    ahead, back = fetch(value, name, 1), fetch(value, name, 3)
    cut = value.shape[0] // 2
    across = jnp.concatenate([fetch(ahead[:cut], name, 1), fetch(back[cut:], name, 3)], 0)
    return [value, ahead, across, back]


def sum_tok_rows(value):
    total = value
    for d in range(1, 4):
        total = total + jnp.roll(fetch(value, "y", d), d, 1)
    return total + jnp.roll(fetch(total, "z", 1), 1, 0)


def gather_tok(value, up, ring):
    other = fetch(value, "z", 1)
    late = value[up:]
    late_y = [fetch(late, "y", d) for d in range(1, 4)]
    early = jnp.stack([value[:up], other[:up]])
    early = ring_slots(early, "y") if ring else [early] + [fetch(early, "y", d) for d in range(1, 4)]
    far = [other[up:]] + [fetch(part, "z", 1) for part in late_y]
    late = [jnp.stack([near, there]) for near, there in zip([late] + late_y, far)]
    return tuple(jnp.stack(part, 1).transpose(2, 0, 1, 3, 4) for part in (early, late))


def sum_tok(near, far, weight, scale):
    def product(part):
        return lax.dot_general(
            part.reshape(-1, part.shape[-1]), weight, (((1,), (0,)), ((), ())), preferred_element_type=F32
        )

    near = near.transpose(3, 2, 0, 1, 4, 5)
    far = far.transpose(2, 3, 0, 1, 4, 5)
    there, near = lax.optimization_barrier((pack(product(far[1]), scale), near))
    there = send(there, "z", 1)
    sent = [send(pack(product(near[d]), scale), "y", d) for d in range(1, 4)]
    near_sum, far_sum = lax.optimization_barrier((product(near[0]), product(far[0])))
    for part in sent:
        near_sum = near_sum + unpack(part, scale)
    near_sum = sum_slots(near_sum.reshape(2, -1, near_sum.shape[-1]), "z", scale)
    far_sum = far_sum + unpack(there, scale)
    far_sum = sum_slots(far_sum.reshape(4, -1, far_sum.shape[-1]), "y", scale)
    return jnp.concatenate([near_sum, far_sum], 0)


def merge(states):
    top = states[0][0]
    for other in states[1:]:
        top = jnp.maximum(top, other[0])
    total, moment, picked = 0.0, 0.0, 0.0
    for state in states:
        below = state[0] - top
        factor = jnp.exp(below)
        total = total + state[1] * factor
        moment = moment + (state[2] + state[1] * below) * factor
        picked = picked + state[3]
    return jnp.stack([top, total, moment, picked])


def softmax_rows(logits, wanted, first_column, rep):
    columns = first_column + lax.broadcasted_iota(jnp.int32, logits.shape, 1)
    target_hit = columns == wanted[:, None]
    picked = jnp.sum(jnp.where(target_hit, logits, 0.0), axis=1)
    top = jnp.max(logits, axis=1)
    below = logits - top[:, None]
    weights = jnp.exp(below)
    total = jnp.sum(weights, axis=1)
    moment = jnp.sum(weights * below, axis=1)
    state = jnp.stack([top, total, moment, picked]).reshape(4, 2, 4, 2, rep)
    for name, dim in (("c", 1), ("x", 2), ("zh", 3)):
        state = merge([state] + [jnp.roll(fetch(state, name, d), d, dim) for d in range(1, AXES[name][2])])
    row_top, row_total, moment, picked = state.reshape(4, -1)
    token_loss = jnp.log(row_total) + row_top - picked
    inner = moment / row_total + (row_top - picked)
    probable = jnp.exp(logits - row_top[:, None]) / row_total[:, None]
    logit_grad = (probable - target_hit.astype(F32)).astype(BF16)
    return token_loss, logit_grad, inner


def body(hidden_rows, join_weight, norm_gain, head_weight, targets):
    tok_index = lax.axis_index("tok")
    voc_index = lax.axis_index("vocab")
    width = join_weight.shape[1]
    full_width = width * 8
    rep = hidden_rows.shape[0]
    depth = join_weight.shape[0]
    own = targets.shape[0] // 8

    def relative(value):
        value = to_relative(to_relative(to_relative(value, 0, "zh"), 1, "x"), 2, "c")
        return value.transpose((2, 1, 0) + tuple(range(3, value.ndim)))

    wanted = lax.dynamic_slice_in_dim(targets, tok_index * own, own, 0)
    wanted = relative(wanted.reshape(2, 4, 2, rep)).reshape(-1)

    spread = lax.all_to_all(hidden_rows, "vocab", split_axis=1, concat_axis=0, tiled=True)
    spread = relative(spread.reshape(2, 4, 2, rep, depth))
    rows = 8 * rep
    inputs = jnp.concatenate(gather_tok(spread.reshape(16, rep, depth), 6, False), 0)
    inputs = inputs.reshape(2, 4, 2, rows, depth)

    joined = sum_vocab(inputs[0], inputs[1], join_weight, (((1,), (0,)), ((), ())), 8.0)
    squares = sum_tok_rows(jnp.sum(joined * joined, axis=1).reshape(2, 4, rep)).reshape(-1)
    inverse_rms = lax.rsqrt(squares / full_width + epsilon)[:, None]
    unit_rows = joined * inverse_rms
    near = gather_x_zh((unit_rows * norm_gain).astype(BF16))
    far = fetch(near, "c", 1)
    near, far = (part.reshape(4, 2, 2, 4, rep, width) for part in (near, far))
    logits = sum_tok(near, far, head_weight, 1.0 / 16)
    token_loss, logit_grad, inner = softmax_rows(logits, wanted, voc_index * head_weight.shape[1], rep)
    token_loss = token_loss.reshape(2, 4, 2, rep).transpose(2, 1, 0, 3)
    token_loss = to_absolute(to_absolute(to_absolute(token_loss, 0, "zh"), 1, "x"), 2, "c").reshape(-1)
    inner = gather_slots(gather_slots(inner[:rep], "y"), "z").reshape(-1, 1)

    left = jnp.pad(inputs, ((0, 0), (0, 0), (0, 0), (0, 8), (0, 0))).reshape(-1, depth)
    grads = [part.reshape(4, 2, rows, -1) for part in gather_tok(logit_grad.reshape(16, rep, -1), 8, True)]
    grads, left = lax.optimization_barrier((grads, left))
    dnormed = sum_vocab(grads[0], grads[1], head_weight, (((1,), (1,)), ((), ())), 1024.0)
    unit_grad = dnormed * norm_gain
    dfused = (inverse_rms * (unit_grad - unit_rows * (inner / full_width))).astype(BF16)

    gain = jnp.sum(dnormed * unit_rows, axis=0)
    pieces = []
    for _ in range(3):
        piece = lax.reduce_precision(gain, 8, 7)
        gain = gain - piece
        pieces.append(piece.astype(BF16))
    extra = jnp.stack(pieces + [jnp.zeros_like(pieces[0])] * 5)
    message = gather_x_zh(jnp.concatenate([dfused, extra], 0))
    message = jnp.stack([message, fetch(message, "c", 1)])
    gain_grad = jnp.sum(message[:, :, :, rows : rows + 3].astype(F32), axis=(0, 1, 2, 3))
    join_grad = lax.dot_general(
        left, message.reshape(-1, width), (((0,), (0,)), ((), ())), preferred_element_type=F32
    )
    return (token_loss, gain_grad, join_grad.astype(BF16))


def solution(mesh):
    placed = (P(("tok", "vocab"), None), P("vocab", "tok"), P("tok"), P("tok", "vocab"), P())
    return jax.shard_map(
        body,
        mesh=mesh,
        in_specs=placed,
        out_specs=(P("tok"), P("tok"), P("vocab", "tok")),
        check_vma=False,
    )
```

```python
import jax
import jax.numpy as jnp
from jax import lax
from jax.sharding import PartitionSpec as P

epsilon = 1e-05
F32, F16, BF16 = jnp.float32, jnp.float16, jnp.bfloat16

AXES = {"z": ("tok", 4, 2), "y": ("tok", 1, 4), "zh": ("vocab", 8, 2), "x": ("vocab", 2, 4), "c": ("vocab", 1, 2)}
SIZE = {"tok": 8, "vocab": 16}


def coord(name):
    axis, stride, size = AXES[name]
    return (lax.axis_index(axis) // stride) % size


def send(value, name, shift):
    axis, stride, size = AXES[name]
    perm = []
    for i in range(SIZE[axis]):
        at = (i // stride) % size
        perm.append((i, i + ((at + shift) % size - at) * stride))
    return lax.ppermute(value, axis, perm)


def fetch(value, name, ahead):
    return send(value, name, -ahead)


def to_relative(value, dim, name):
    size = AXES[name][2]
    return lax.dynamic_slice_in_dim(jnp.concatenate([value, value], dim), coord(name), size, dim)


def to_absolute(value, dim, name):
    size = AXES[name][2]
    return lax.dynamic_slice_in_dim(jnp.concatenate([value, value], dim), size - coord(name), size, dim)


def pack(value, scale):
    return (value * scale).astype(F16)


def unpack(value, scale):
    return value.astype(F32) * (1.0 / scale)


def sum_slots(value, name, scale):
    sent = [send(pack(value[d], scale), name, d) for d in range(1, AXES[name][2])]
    total = value[0]
    for part in sent:
        total = total + unpack(part, scale)
    return total


def gather_slots(value, name):
    return jnp.stack([value] + [fetch(value, name, d) for d in range(1, AXES[name][2])])


def sum_vocab(near, far, weight, dims, scale, apart):
    nx, nh, rows, depth = near.shape

    def product(part):
        return lax.dot_general(part.reshape(-1, depth), weight, dims, preferred_element_type=F32)

    theirs = send(pack(product(far), scale), "c", 1)
    if not apart:
        ours = product(near) + unpack(theirs, scale)
        ours = sum_slots(ours.reshape(nx, nh, rows, -1), "x", scale)
        return sum_slots(ours, "zh", scale)
    cut = nh * rows
    theirs = [unpack(theirs[d * cut : (d + 1) * cut], scale) for d in range(nx)]
    others = product(near[1:]).reshape(nx - 1, cut, -1)
    sent = [send(pack(others[d - 1] + theirs[d], scale), "x", d) for d in range(1, nx)]
    ours = product(near[0]) + theirs[0]
    for part in sent:
        ours = ours + unpack(part, scale)
    return sum_slots(ours.reshape(nh, rows, -1), "zh", scale)


def gather_vocab(value):
    value = gather_slots(value, "zh")
    slots = [value] + [fetch(value, "x", d) for d in range(1, 4)]
    return jnp.stack(slots), jnp.stack([fetch(slot, "c", 1) for slot in slots])


def ring_slots(value, name):
    ahead, back = fetch(value, name, 1), fetch(value, name, 3)
    cut = value.shape[0] // 2
    across = jnp.concatenate([fetch(ahead[:cut], name, 1), fetch(back[cut:], name, 3)], 0)
    return [value, ahead, across, back]


def sum_tok_rows(value):
    total = value
    for d in range(1, 4):
        total = total + jnp.roll(fetch(value, "y", d), d, 1)
    return total + jnp.roll(fetch(total, "z", 1), 1, 0)


def gather_tok(value, up, ring):
    other = fetch(value, "z", 1)
    late = value[up:]
    late_y = [fetch(late, "y", d) for d in range(1, 4)]
    early = jnp.stack([value[:up], other[:up]])
    early = ring_slots(early, "y") if ring else [early] + [fetch(early, "y", d) for d in range(1, 4)]
    far = [other[up:]] + [fetch(part, "z", 1) for part in late_y]
    late = [jnp.stack([near, there]) for near, there in zip([late] + late_y, far)]
    return tuple(jnp.stack(part, 1).transpose(2, 0, 1, 3, 4) for part in (early, late))


def sum_tok(near, far, weight, scale):
    def product(part):
        return lax.dot_general(
            part.reshape(-1, part.shape[-1]), weight, (((1,), (0,)), ((), ())), preferred_element_type=F32
        )

    near = near.transpose(3, 2, 0, 1, 4, 5)
    far = far.transpose(2, 3, 0, 1, 4, 5)
    there, near = lax.optimization_barrier((pack(product(far[1]), scale), near))
    there = send(there, "z", 1)
    sent = [send(pack(product(near[d]), scale), "y", d) for d in range(1, 4)]
    near_sum, far_sum = lax.optimization_barrier((product(near[0]), product(far[0])))
    for part in sent:
        near_sum = near_sum + unpack(part, scale)
    near_sum = sum_slots(near_sum.reshape(2, -1, near_sum.shape[-1]), "z", scale)
    far_sum = far_sum + unpack(there, scale)
    far_sum = sum_slots(far_sum.reshape(4, -1, far_sum.shape[-1]), "y", scale)
    return jnp.concatenate([near_sum, far_sum], 0)


def merge(states):
    top = states[0][0]
    for other in states[1:]:
        top = jnp.maximum(top, other[0])
    total, moment, picked = 0.0, 0.0, 0.0
    for state in states:
        below = state[0] - top
        factor = jnp.exp(below)
        total = total + state[1] * factor
        moment = moment + (state[2] + state[1] * below) * factor
        picked = picked + state[3]
    return jnp.stack([top, total, moment, picked])


def softmax_rows(logits, wanted, first_column, rep):
    columns = first_column + lax.broadcasted_iota(jnp.int32, logits.shape, 1)
    target_hit = columns == wanted[:, None]
    picked = jnp.sum(jnp.where(target_hit, logits, 0.0), axis=1)
    top = jnp.max(logits, axis=1)
    below = logits - top[:, None]
    weights = jnp.exp(below)
    total = jnp.sum(weights, axis=1)
    moment = jnp.sum(weights * below, axis=1)
    state = jnp.stack([top, total, moment, picked]).reshape(4, 2, 4, 2, rep)
    for name, dim in (("c", 1), ("x", 2), ("zh", 3)):
        state = merge([state] + [jnp.roll(fetch(state, name, d), d, dim) for d in range(1, AXES[name][2])])
    row_top, row_total, moment, picked = state.reshape(4, -1)
    token_loss = jnp.log(row_total) + row_top - picked
    inner = moment / row_total + (row_top - picked)
    probable = jnp.exp(logits - row_top[:, None]) / row_total[:, None]
    logit_grad = (probable - target_hit.astype(F32)).astype(BF16)
    return token_loss, logit_grad, inner


def body(hidden_rows, join_weight, norm_gain, head_weight, targets):
    tok_index = lax.axis_index("tok")
    voc_index = lax.axis_index("vocab")
    width = join_weight.shape[1]
    full_width = width * 8
    rep = hidden_rows.shape[0]
    depth = join_weight.shape[0]
    own = targets.shape[0] // 8

    def relative(value):
        value = to_relative(to_relative(to_relative(value, 0, "zh"), 1, "x"), 2, "c")
        return value.transpose((2, 1, 0) + tuple(range(3, value.ndim)))

    wanted = lax.dynamic_slice_in_dim(targets, tok_index * own, own, 0)
    wanted = relative(wanted.reshape(2, 4, 2, rep)).reshape(-1)

    spread = lax.all_to_all(hidden_rows, "vocab", split_axis=1, concat_axis=0, tiled=True)
    spread = relative(spread.reshape(2, 4, 2, rep, depth))
    rows = 8 * rep
    inputs = jnp.concatenate(gather_tok(spread.reshape(16, rep, depth), 6, False), 0)
    inputs = inputs.reshape(2, 4, 2, rows, depth)

    joined = sum_vocab(inputs[0], inputs[1], join_weight, (((1,), (0,)), ((), ())), 8.0, True)
    squares = sum_tok_rows(jnp.sum(joined * joined, axis=1).reshape(2, 4, rep)).reshape(-1)
    inverse_rms = lax.rsqrt(squares / full_width + epsilon)[:, None]
    unit_rows = joined * inverse_rms
    normed = gather_vocab((unit_rows * norm_gain).astype(BF16))
    near, far = (part.reshape(4, 2, 2, 4, rep, width) for part in normed)
    logits = sum_tok(near, far, head_weight, 1.0 / 16)
    token_loss, logit_grad, inner = softmax_rows(logits, wanted, voc_index * head_weight.shape[1], rep)
    token_loss = token_loss.reshape(2, 4, 2, rep).transpose(2, 1, 0, 3)
    token_loss = to_absolute(to_absolute(to_absolute(token_loss, 0, "zh"), 1, "x"), 2, "c").reshape(-1)
    inner = gather_slots(gather_slots(inner[:rep], "y"), "z").reshape(-1, 1)

    left = jnp.pad(inputs, ((0, 0), (0, 0), (0, 0), (0, 8), (0, 0))).reshape(-1, depth)
    grads = [part.reshape(4, 2, rows, -1) for part in gather_tok(logit_grad.reshape(16, rep, -1), 8, True)]
    grads[1], left = lax.optimization_barrier((grads[1], left))
    dnormed = sum_vocab(grads[0], grads[1], head_weight, (((1,), (1,)), ((), ())), 1024.0, False)
    unit_grad = dnormed * norm_gain
    dfused = (inverse_rms * (unit_grad - unit_rows * (inner / full_width))).astype(BF16)

    gain = jnp.sum(dnormed * unit_rows, axis=0)
    pieces = []
    for _ in range(3):
        piece = lax.reduce_precision(gain, 8, 7)
        gain = gain - piece
        pieces.append(piece.astype(BF16))
    extra = jnp.stack(pieces + [jnp.zeros_like(pieces[0])] * 5)
    message = jnp.stack(gather_vocab(jnp.concatenate([dfused, extra], 0)))
    gain_grad = jnp.sum(message[:, :, :, rows : rows + 3].astype(F32), axis=(0, 1, 2, 3))
    join_grad = lax.dot_general(
        left, message.reshape(-1, width), (((0,), (0,)), ((), ())), preferred_element_type=F32
    )
    return (token_loss, gain_grad, join_grad.astype(BF16))


def solution(mesh):
    placed = (P(("tok", "vocab"), None), P("vocab", "tok"), P("tok"), P("tok", "vocab"), P())
    return jax.shard_map(
        body,
        mesh=mesh,
        in_specs=placed,
        out_specs=(P("tok"), P("tok"), P("vocab", "tok")),
        check_vma=False,
    )
```

```python
import jax
import jax.numpy as jnp
from jax import lax
from jax.sharding import PartitionSpec as P

epsilon = 1e-05
F32, F16, BF16 = jnp.float32, jnp.float16, jnp.bfloat16

AXES = {"z": ("tok", 4, 2), "y": ("tok", 1, 4), "zh": ("vocab", 8, 2), "x": ("vocab", 2, 4), "c": ("vocab", 1, 2)}
SIZE = {"tok": 8, "vocab": 16}


def coord(name):
    axis, stride, size = AXES[name]
    return (lax.axis_index(axis) // stride) % size


def send(value, name, shift):
    axis, stride, size = AXES[name]
    perm = []
    for i in range(SIZE[axis]):
        at = (i // stride) % size
        perm.append((i, i + ((at + shift) % size - at) * stride))
    return lax.ppermute(value, axis, perm)


def fetch(value, name, ahead):
    return send(value, name, -ahead)


def to_relative(value, dim, name):
    size = AXES[name][2]
    return lax.dynamic_slice_in_dim(jnp.concatenate([value, value], dim), coord(name), size, dim)


def to_absolute(value, dim, name):
    size = AXES[name][2]
    return lax.dynamic_slice_in_dim(jnp.concatenate([value, value], dim), size - coord(name), size, dim)


def pack(value, scale):
    return (value * scale).astype(F16)


def unpack(value, scale):
    return value.astype(F32) * (1.0 / scale)


def sum_slots(value, name, scale):
    sent = [send(pack(value[d], scale), name, d) for d in range(1, AXES[name][2])]
    total = value[0]
    for part in sent:
        total = total + unpack(part, scale)
    return total


def gather_slots(value, name):
    return jnp.stack([value] + [fetch(value, name, d) for d in range(1, AXES[name][2])])


def sum_vocab(near, far, weight, dims, scale, apart):
    nx, nh, rows, depth = near.shape

    def product(part):
        return lax.dot_general(part.reshape(-1, depth), weight, dims, preferred_element_type=F32)

    theirs = send(pack(product(far), scale), "c", 1)
    if not apart:
        ours = product(near) + unpack(theirs, scale)
        ours = sum_slots(ours.reshape(nx, nh, rows, -1), "x", scale)
        return sum_slots(ours, "zh", scale)
    theirs = theirs.reshape(nx, nh, rows, -1)
    others = product(near[1:]).reshape(nx - 1, nh, rows, -1)
    sent = [
        [send(pack(others[d - 1, h] + unpack(theirs[d, h], scale), scale), "x", d) for d in range(1, nx)]
        for h in (1, 0)
    ]
    ours = product(near[0]).reshape(nh, rows, -1) + unpack(theirs[0], scale)
    away, ours = ours[1], ours[0]
    for part in sent[0]:
        away = away + unpack(part, scale)
    away = send(pack(away, scale), "zh", 1)
    for part in sent[1] + [away]:
        ours = ours + unpack(part, scale)
    return ours


def gather_vocab(value):
    other = fetch(value, "zh", 1)
    first = [value] + [fetch(value, "x", d) for d in range(1, 4)]
    second = [other] + [fetch(other, "x", d) for d in range(1, 4)]
    first_far = fetch(jnp.stack(first), "c", 1)
    second_far = jnp.stack([fetch(slot, "c", 1) for slot in second])
    return jnp.stack([jnp.stack(first), jnp.stack(second)], 1), jnp.stack([first_far, second_far], 1)


def ring_slots(value, name):
    ahead, back = fetch(value, name, 1), fetch(value, name, 3)
    cut = value.shape[0] // 2
    across = jnp.concatenate([fetch(ahead[:cut], name, 1), fetch(back[cut:], name, 3)], 0)
    return [value, ahead, across, back]


def sum_tok_rows(value):
    total = value
    for d in range(1, 4):
        total = total + jnp.roll(fetch(value, "y", d), d, 1)
    return total + jnp.roll(fetch(total, "z", 1), 1, 0)


def gather_tok(value, up, ring):
    other = fetch(value, "z", 1)
    late = value[up:]
    late_y = [fetch(late, "y", d) for d in range(1, 4)]
    early = jnp.stack([value[:up], other[:up]])
    early = ring_slots(early, "y") if ring else [early] + [fetch(early, "y", d) for d in range(1, 4)]
    far = [other[up:]] + [fetch(part, "z", 1) for part in late_y]
    late = [jnp.stack([near, there]) for near, there in zip([late] + late_y, far)]
    return tuple(jnp.stack(part, 1).transpose(2, 0, 1, 3, 4) for part in (early, late))


def sum_tok(near, far, weight, scale):
    def product(part):
        return lax.dot_general(
            part.reshape(-1, part.shape[-1]), weight, (((1,), (0,)), ((), ())), preferred_element_type=F32
        )

    near = near.transpose(3, 2, 0, 1, 4, 5)
    far = far.transpose(2, 3, 0, 1, 4, 5)
    there, near = lax.optimization_barrier((pack(product(far[1]), scale), near))
    there = send(there, "z", 1)
    sent = [send(pack(product(near[d]), scale), "y", d) for d in range(1, 4)]
    near_sum, far_sum = lax.optimization_barrier((product(near[0]), product(far[0])))
    for part in sent:
        near_sum = near_sum + unpack(part, scale)
    near_sum = sum_slots(near_sum.reshape(2, -1, near_sum.shape[-1]), "z", scale)
    far_sum = far_sum + unpack(there, scale)
    far_sum = sum_slots(far_sum.reshape(4, -1, far_sum.shape[-1]), "y", scale)
    return jnp.concatenate([near_sum, far_sum], 0)


def merge(states):
    top = states[0][0]
    for other in states[1:]:
        top = jnp.maximum(top, other[0])
    total, moment, picked = 0.0, 0.0, 0.0
    for state in states:
        below = state[0] - top
        factor = jnp.exp(below)
        total = total + state[1] * factor
        moment = moment + (state[2] + state[1] * below) * factor
        picked = picked + state[3]
    return jnp.stack([top, total, moment, picked])


def softmax_rows(logits, wanted, first_column, rep):
    columns = first_column + lax.broadcasted_iota(jnp.int32, logits.shape, 1)
    target_hit = columns == wanted[:, None]
    picked = jnp.sum(jnp.where(target_hit, logits, 0.0), axis=1)
    top = jnp.max(logits, axis=1)
    below = logits - top[:, None]
    weights = jnp.exp(below)
    total = jnp.sum(weights, axis=1)
    moment = jnp.sum(weights * below, axis=1)
    state = jnp.stack([top, total, moment, picked]).reshape(4, 2, 4, 2, rep)
    for name, dim in (("c", 1), ("x", 2), ("zh", 3)):
        state = merge([state] + [jnp.roll(fetch(state, name, d), d, dim) for d in range(1, AXES[name][2])])
    row_top, row_total, moment, picked = state.reshape(4, -1)
    token_loss = jnp.log(row_total) + row_top - picked
    inner = moment / row_total + (row_top - picked)
    probable = jnp.exp(logits - row_top[:, None]) / row_total[:, None]
    logit_grad = (probable - target_hit.astype(F32)).astype(BF16)
    return token_loss, logit_grad, inner


def body(hidden_rows, join_weight, norm_gain, head_weight, targets):
    tok_index = lax.axis_index("tok")
    voc_index = lax.axis_index("vocab")
    width = join_weight.shape[1]
    full_width = width * 8
    rep = hidden_rows.shape[0]
    depth = join_weight.shape[0]
    own = targets.shape[0] // 8

    def relative(value):
        value = to_relative(to_relative(to_relative(value, 0, "zh"), 1, "x"), 2, "c")
        return value.transpose((2, 1, 0) + tuple(range(3, value.ndim)))

    wanted = lax.dynamic_slice_in_dim(targets, tok_index * own, own, 0)
    wanted = relative(wanted.reshape(2, 4, 2, rep)).reshape(-1)

    spread = lax.all_to_all(hidden_rows, "vocab", split_axis=1, concat_axis=0, tiled=True)
    spread = relative(spread.reshape(2, 4, 2, rep, depth))
    rows = 8 * rep
    inputs = jnp.concatenate(gather_tok(spread.reshape(16, rep, depth), 6, False), 0)
    inputs = inputs.reshape(2, 4, 2, rows, depth)

    joined = sum_vocab(inputs[0], inputs[1], join_weight, (((1,), (0,)), ((), ())), 8.0, True)
    squares = sum_tok_rows(jnp.sum(joined * joined, axis=1).reshape(2, 4, rep)).reshape(-1)
    inverse_rms = lax.rsqrt(squares / full_width + epsilon)[:, None]
    unit_rows = joined * inverse_rms
    normed = gather_vocab((unit_rows * norm_gain).astype(BF16))
    near, far = (part.reshape(4, 2, 2, 4, rep, width) for part in normed)
    logits = sum_tok(near, far, head_weight, 1.0 / 16)
    token_loss, logit_grad, inner = softmax_rows(logits, wanted, voc_index * head_weight.shape[1], rep)
    token_loss = token_loss.reshape(2, 4, 2, rep).transpose(2, 1, 0, 3)
    token_loss = to_absolute(to_absolute(to_absolute(token_loss, 0, "zh"), 1, "x"), 2, "c").reshape(-1)
    inner = gather_slots(gather_slots(inner[:rep], "y"), "z").reshape(-1, 1)

    left = jnp.pad(inputs, ((0, 0), (0, 0), (0, 0), (0, 8), (0, 0))).reshape(-1, depth)
    grads = [part.reshape(4, 2, rows, -1) for part in gather_tok(logit_grad.reshape(16, rep, -1), 8, True)]
    grads[1], left = lax.optimization_barrier((grads[1], left))
    dnormed = sum_vocab(grads[0], grads[1], head_weight, (((1,), (1,)), ((), ())), 1024.0, False)
    unit_grad = dnormed * norm_gain
    dfused = (inverse_rms * (unit_grad - unit_rows * (inner / full_width))).astype(BF16)

    gain = jnp.sum(dnormed * unit_rows, axis=0)
    pieces = []
    for _ in range(3):
        piece = lax.reduce_precision(gain, 8, 7)
        gain = gain - piece
        pieces.append(piece.astype(BF16))
    extra = jnp.stack(pieces + [jnp.zeros_like(pieces[0])] * 5)
    message = jnp.stack(gather_vocab(jnp.concatenate([dfused, extra], 0)))
    gain_grad = jnp.sum(message[:, :, :, rows : rows + 3].astype(F32), axis=(0, 1, 2, 3))
    join_grad = lax.dot_general(
        left, message.reshape(-1, width), (((0,), (0,)), ((), ())), preferred_element_type=F32
    )
    return (token_loss, gain_grad, join_grad.astype(BF16))


def solution(mesh):
    placed = (P(("tok", "vocab"), None), P("vocab", "tok"), P("tok"), P("tok", "vocab"), P())
    return jax.shard_map(
        body,
        mesh=mesh,
        in_specs=placed,
        out_specs=(P("tok"), P("tok"), P("vocab", "tok")),
        check_vma=False,
    )
```

```python
import jax
import jax.numpy as jnp
from jax import lax
from jax.sharding import PartitionSpec as P

epsilon = 1e-05
F32, F16, BF16 = jnp.float32, jnp.float16, jnp.bfloat16

AXES = {"z": ("tok", 4, 2), "y": ("tok", 1, 4), "zh": ("vocab", 8, 2), "x": ("vocab", 2, 4), "c": ("vocab", 1, 2)}
SIZE = {"tok": 8, "vocab": 16}


def coord(name):
    axis, stride, size = AXES[name]
    return (lax.axis_index(axis) // stride) % size


def send(value, name, shift):
    axis, stride, size = AXES[name]
    perm = []
    for i in range(SIZE[axis]):
        at = (i // stride) % size
        perm.append((i, i + ((at + shift) % size - at) * stride))
    return lax.ppermute(value, axis, perm)


def fetch(value, name, ahead):
    return send(value, name, -ahead)


def to_relative(value, dim, name):
    size = AXES[name][2]
    return lax.dynamic_slice_in_dim(jnp.concatenate([value, value], dim), coord(name), size, dim)


def to_absolute(value, dim, name):
    size = AXES[name][2]
    return lax.dynamic_slice_in_dim(jnp.concatenate([value, value], dim), size - coord(name), size, dim)


def pack(value, scale):
    return (value * scale).astype(F16)


def unpack(value, scale):
    return value.astype(F32) * (1.0 / scale)


def sum_slots(value, name, scale):
    sent = [send(pack(value[d], scale), name, d) for d in range(1, AXES[name][2])]
    total = value[0]
    for part in sent:
        total = total + unpack(part, scale)
    return total


def gather_slots(value, name):
    return jnp.stack([value] + [fetch(value, name, d) for d in range(1, AXES[name][2])])


def sum_vocab(near, far, weight, dims, scale, apart):
    nx, nh, rows, depth = near.shape

    def product(part):
        return lax.dot_general(part.reshape(-1, depth), weight, dims, preferred_element_type=F32)

    theirs = send(pack(product(far), scale), "c", 1)
    if not apart:
        ours = (product(near) + unpack(theirs, scale)).reshape(nx, nh, rows, -1)
        away = sum_slots(ours[:, 1], "x", scale)
        return sum_slots(ours[:, 0], "x", scale) + unpack(send(pack(away, scale), "zh", 1), scale)
    theirs = theirs.reshape(nx, nh, rows, -1)
    others = product(near[1:]).reshape(nx - 1, nh, rows, -1)
    sent = [
        [send(pack(others[d - 1, h] + unpack(theirs[d, h], scale), scale), "x", d) for d in range(1, nx)]
        for h in (1, 0)
    ]
    ours = product(near[0]).reshape(nh, rows, -1) + unpack(theirs[0], scale)
    away, ours = ours[1], ours[0]
    for part in sent[0]:
        away = away + unpack(part, scale)
    away = send(pack(away, scale), "zh", 1)
    for part in sent[1] + [away]:
        ours = ours + unpack(part, scale)
    return ours


def gather_vocab(value):
    other = fetch(value, "zh", 1)
    first = [value] + [fetch(value, "x", d) for d in range(1, 4)]
    second = [other] + [fetch(other, "x", d) for d in range(1, 4)]
    first_far = fetch(jnp.stack(first), "c", 1)
    second_far = jnp.stack([fetch(slot, "c", 1) for slot in second])
    return jnp.stack([jnp.stack(first), jnp.stack(second)], 1), jnp.stack([first_far, second_far], 1)


def ring_slots(value, name):
    ahead, back = fetch(value, name, 1), fetch(value, name, 3)
    cut = value.shape[0] // 2
    across = jnp.concatenate([fetch(ahead[:cut], name, 1), fetch(back[cut:], name, 3)], 0)
    return [value, ahead, across, back]


def sum_tok_rows(value):
    total = value
    for d in range(1, 4):
        total = total + jnp.roll(fetch(value, "y", d), d, 1)
    return total + jnp.roll(fetch(total, "z", 1), 1, 0)


def gather_tok(value, up, ring):
    other = fetch(value, "z", 1)
    late = value[up:]
    late_y = [fetch(late, "y", d) for d in range(1, 4)]
    early = jnp.stack([value[:up], other[:up]])
    early = ring_slots(early, "y") if ring else [early] + [fetch(early, "y", d) for d in range(1, 4)]
    far = [other[up:]] + [fetch(part, "z", 1) for part in late_y]
    late = [jnp.stack([near, there]) for near, there in zip([late] + late_y, far)]
    return tuple(jnp.stack(part, 1).transpose(2, 0, 1, 3, 4) for part in (early, late))


def sum_tok(near, far, weight, scale):
    def product(part):
        return lax.dot_general(
            part.reshape(-1, part.shape[-1]), weight, (((1,), (0,)), ((), ())), preferred_element_type=F32
        )

    near = near.transpose(3, 2, 0, 1, 4, 5)
    far = far.transpose(2, 3, 0, 1, 4, 5)
    there, near = lax.optimization_barrier((pack(product(far[1]), scale), near))
    there = send(there, "z", 1)
    sent = [send(pack(product(near[d]), scale), "y", d) for d in range(1, 4)]
    near_sum, far_sum = lax.optimization_barrier((product(near[0]), product(far[0])))
    for part in sent:
        near_sum = near_sum + unpack(part, scale)
    near_sum = sum_slots(near_sum.reshape(2, -1, near_sum.shape[-1]), "z", scale)
    far_sum = far_sum + unpack(there, scale)
    far_sum = sum_slots(far_sum.reshape(4, -1, far_sum.shape[-1]), "y", scale)
    return jnp.concatenate([near_sum, far_sum], 0)


def merge(states):
    top = states[0][0]
    for other in states[1:]:
        top = jnp.maximum(top, other[0])
    total, moment, picked = 0.0, 0.0, 0.0
    for state in states:
        below = state[0] - top
        factor = jnp.exp(below)
        total = total + state[1] * factor
        moment = moment + (state[2] + state[1] * below) * factor
        picked = picked + state[3]
    return jnp.stack([top, total, moment, picked])


def softmax_rows(logits, wanted, first_column, rep):
    columns = first_column + lax.broadcasted_iota(jnp.int32, logits.shape, 1)
    target_hit = columns == wanted[:, None]
    picked = jnp.sum(jnp.where(target_hit, logits, 0.0), axis=1)
    top = jnp.max(logits, axis=1)
    below = logits - top[:, None]
    weights = jnp.exp(below)
    total = jnp.sum(weights, axis=1)
    moment = jnp.sum(weights * below, axis=1)
    state = jnp.stack([top, total, moment, picked]).reshape(4, 2, 4, 2, rep)
    for name, dim in (("c", 1), ("x", 2), ("zh", 3)):
        state = merge([state] + [jnp.roll(fetch(state, name, d), d, dim) for d in range(1, AXES[name][2])])
    row_top, row_total, moment, picked = state.reshape(4, -1)
    token_loss = jnp.log(row_total) + row_top - picked
    inner = moment / row_total + (row_top - picked)
    probable = jnp.exp(logits - row_top[:, None]) / row_total[:, None]
    logit_grad = (probable - target_hit.astype(F32)).astype(BF16)
    return token_loss, logit_grad, inner


def body(hidden_rows, join_weight, norm_gain, head_weight, targets):
    tok_index = lax.axis_index("tok")
    voc_index = lax.axis_index("vocab")
    width = join_weight.shape[1]
    full_width = width * 8
    rep = hidden_rows.shape[0]
    depth = join_weight.shape[0]
    own = targets.shape[0] // 8

    def relative(value):
        value = to_relative(to_relative(to_relative(value, 0, "zh"), 1, "x"), 2, "c")
        return value.transpose((2, 1, 0) + tuple(range(3, value.ndim)))

    wanted = lax.dynamic_slice_in_dim(targets, tok_index * own, own, 0)
    wanted = relative(wanted.reshape(2, 4, 2, rep)).reshape(-1)

    spread = lax.all_to_all(hidden_rows, "vocab", split_axis=1, concat_axis=0, tiled=True)
    spread = relative(spread.reshape(2, 4, 2, rep, depth))
    rows = 8 * rep
    inputs = jnp.concatenate(gather_tok(spread.reshape(16, rep, depth), 6, False), 0)
    inputs = inputs.reshape(2, 4, 2, rows, depth)

    joined = sum_vocab(inputs[0], inputs[1], join_weight, (((1,), (0,)), ((), ())), 8.0, True)
    squares = sum_tok_rows(jnp.sum(joined * joined, axis=1).reshape(2, 4, rep)).reshape(-1)
    inverse_rms = lax.rsqrt(squares / full_width + epsilon)[:, None]
    unit_rows = joined * inverse_rms
    normed = gather_vocab((unit_rows * norm_gain).astype(BF16))
    near, far = (part.reshape(4, 2, 2, 4, rep, width) for part in normed)
    logits = sum_tok(near, far, head_weight, 1.0 / 16)
    token_loss, logit_grad, inner = softmax_rows(logits, wanted, voc_index * head_weight.shape[1], rep)
    token_loss = token_loss.reshape(2, 4, 2, rep).transpose(2, 1, 0, 3)
    token_loss = to_absolute(to_absolute(to_absolute(token_loss, 0, "zh"), 1, "x"), 2, "c").reshape(-1)
    inner = gather_slots(gather_slots(inner[:rep], "y"), "z").reshape(-1, 1)

    left = jnp.pad(inputs, ((0, 0), (0, 0), (0, 0), (0, 8), (0, 0))).reshape(-1, depth)
    grads = [part.reshape(4, 2, rows, -1) for part in gather_tok(logit_grad.reshape(16, rep, -1), 8, True)]
    grads[1], left = lax.optimization_barrier((grads[1], left))
    dnormed = sum_vocab(grads[0], grads[1], head_weight, (((1,), (1,)), ((), ())), 1024.0, False)
    unit_grad = dnormed * norm_gain
    dfused = (inverse_rms * (unit_grad - unit_rows * (inner / full_width))).astype(BF16)

    gain = jnp.sum(dnormed * unit_rows, axis=0)
    pieces = []
    for _ in range(3):
        piece = lax.reduce_precision(gain, 8, 7)
        gain = gain - piece
        pieces.append(piece.astype(BF16))
    extra = jnp.stack(pieces + [jnp.zeros_like(pieces[0])] * 5)
    message = jnp.stack(gather_vocab(jnp.concatenate([dfused, extra], 0)))
    gain_grad = jnp.sum(message[:, :, :, rows : rows + 3].astype(F32), axis=(0, 1, 2, 3))
    join_grad = lax.dot_general(
        left, message.reshape(-1, width), (((0,), (0,)), ((), ())), preferred_element_type=F32
    )
    return (token_loss, gain_grad, join_grad.astype(BF16))


def solution(mesh):
    placed = (P(("tok", "vocab"), None), P("vocab", "tok"), P("tok"), P("tok", "vocab"), P())
    return jax.shard_map(
        body,
        mesh=mesh,
        in_specs=placed,
        out_specs=(P("tok"), P("tok"), P("vocab", "tok")),
        check_vma=False,
    )
```

```python
import jax
import jax.numpy as jnp
from jax import lax
from jax.sharding import PartitionSpec as P

epsilon = 1e-05
F32, F16, BF16 = jnp.float32, jnp.float16, jnp.bfloat16

AXES = {"z": ("tok", 4, 2), "y": ("tok", 1, 4), "zh": ("vocab", 8, 2), "x": ("vocab", 2, 4), "c": ("vocab", 1, 2)}
SIZE = {"tok": 8, "vocab": 16}


def coord(name):
    axis, stride, size = AXES[name]
    return (lax.axis_index(axis) // stride) % size


def send(value, name, shift):
    axis, stride, size = AXES[name]
    perm = []
    for i in range(SIZE[axis]):
        at = (i // stride) % size
        perm.append((i, i + ((at + shift) % size - at) * stride))
    return lax.ppermute(value, axis, perm)


def fetch(value, name, ahead):
    return send(value, name, -ahead)


def to_relative(value, dim, name):
    size = AXES[name][2]
    return lax.dynamic_slice_in_dim(jnp.concatenate([value, value], dim), coord(name), size, dim)


def to_absolute(value, dim, name):
    size = AXES[name][2]
    return lax.dynamic_slice_in_dim(jnp.concatenate([value, value], dim), size - coord(name), size, dim)


def pack(value, scale):
    return (value * scale).astype(F16)


def unpack(value, scale):
    return value.astype(F32) * (1.0 / scale)


def sum_slots(value, name, scale):
    sent = [send(pack(value[d], scale), name, d) for d in range(1, AXES[name][2])]
    total = value[0]
    for part in sent:
        total = total + unpack(part, scale)
    return total


def gather_slots(value, name):
    return jnp.stack([value] + [fetch(value, name, d) for d in range(1, AXES[name][2])])


def sum_vocab(near, far, weight, dims, scale, apart):
    nx, nh, rows, depth = near.shape

    def product(part):
        return lax.dot_general(part.reshape(-1, depth), weight, dims, preferred_element_type=F32)

    theirs = send(pack(product(far), scale), "c", 1)
    if not apart:
        ours = (product(near) + unpack(theirs, scale)).reshape(nx, nh, rows, -1)
        away = sum_slots(ours[:, 1], "x", scale)
        return sum_slots(ours[:, 0], "x", scale) + unpack(send(pack(away, scale), "zh", 1), scale)
    theirs = theirs.reshape(nx, nh, rows, -1)
    others = product(near[1:]).reshape(nx - 1, nh, rows, -1)
    sent = [
        [send(pack(others[d - 1, h] + unpack(theirs[d, h], scale), scale), "x", d) for d in range(1, nx)]
        for h in (1, 0)
    ]
    ours = product(near[0]).reshape(nh, rows, -1) + unpack(theirs[0], scale)
    away, ours = ours[1], ours[0]
    for part in sent[0]:
        away = away + unpack(part, scale)
    away = send(pack(away, scale), "zh", 1)
    for part in sent[1] + [away]:
        ours = ours + unpack(part, scale)
    return ours


def gather_vocab(value):
    other = fetch(value, "zh", 1)
    first = [value] + [fetch(value, "x", d) for d in range(1, 4)]
    second = [other] + [fetch(other, "x", d) for d in range(1, 4)]
    first_far = fetch(jnp.stack(first), "c", 1)
    second_far = jnp.stack([fetch(slot, "c", 1) for slot in second])
    return jnp.stack([jnp.stack(first), jnp.stack(second)], 1), jnp.stack([first_far, second_far], 1)


def ring_slots(value, name):
    ahead, back = fetch(value, name, 1), fetch(value, name, 3)
    cut = value.shape[0] // 2
    across = jnp.concatenate([fetch(ahead[:cut], name, 1), fetch(back[cut:], name, 3)], 0)
    return [value, ahead, across, back]


def sum_tok_rows(value):
    total = value
    for d in range(1, 4):
        total = total + jnp.roll(fetch(value, "y", d), d, 1)
    return total + jnp.roll(fetch(total, "z", 1), 1, 0)


def gather_tok(value, up, ring):
    if ring:
        other_early, other_late = fetch(value[:up], "z", 1), fetch(value[up:], "z", 1)
    else:
        other = fetch(value, "z", 1)
        other_early, other_late = other[:up], other[up:]
    late = value[up:]
    late_y = [fetch(late, "y", d) for d in range(1, 4)]
    early = jnp.stack([value[:up], other_early])
    early = ring_slots(early, "y") if ring else [early] + [fetch(early, "y", d) for d in range(1, 4)]
    far = [other_late] + [fetch(part, "z", 1) for part in late_y]
    late = [jnp.stack([near, there]) for near, there in zip([late] + late_y, far)]
    return tuple(jnp.stack(part, 1).transpose(2, 0, 1, 3, 4) for part in (early, late))


def sum_tok(near, far, weight, scale):
    def product(part):
        return lax.dot_general(
            part.reshape(-1, part.shape[-1]), weight, (((1,), (0,)), ((), ())), preferred_element_type=F32
        )

    near = near.transpose(3, 2, 0, 1, 4, 5)
    far = far.transpose(2, 3, 0, 1, 4, 5)
    there, near = lax.optimization_barrier((pack(product(far[1]), scale), near))
    there = send(there, "z", 1)
    sent = [send(pack(product(near[d]), scale), "y", d) for d in range(1, 4)]
    near_sum, far_sum = lax.optimization_barrier((product(near[0]), product(far[0])))
    for part in sent:
        near_sum = near_sum + unpack(part, scale)
    near_sum = sum_slots(near_sum.reshape(2, -1, near_sum.shape[-1]), "z", scale)
    far_sum = far_sum + unpack(there, scale)
    far_sum = sum_slots(far_sum.reshape(4, -1, far_sum.shape[-1]), "y", scale)
    return jnp.concatenate([near_sum, far_sum], 0)


def merge(states):
    top = states[0][0]
    for other in states[1:]:
        top = jnp.maximum(top, other[0])
    total, moment, picked = 0.0, 0.0, 0.0
    for state in states:
        below = state[0] - top
        factor = jnp.exp(below)
        total = total + state[1] * factor
        moment = moment + (state[2] + state[1] * below) * factor
        picked = picked + state[3]
    return jnp.stack([top, total, moment, picked])


def softmax_rows(logits, wanted, first_column, rep):
    columns = first_column + lax.broadcasted_iota(jnp.int32, logits.shape, 1)
    target_hit = columns == wanted[:, None]
    picked = jnp.sum(jnp.where(target_hit, logits, 0.0), axis=1)
    top = jnp.max(logits, axis=1)
    below = logits - top[:, None]
    weights = jnp.exp(below)
    total = jnp.sum(weights, axis=1)
    moment = jnp.sum(weights * below, axis=1)
    state = jnp.stack([top, total, moment, picked]).reshape(4, 2, 4, 2, rep)
    for name, dim in (("c", 1), ("x", 2), ("zh", 3)):
        state = merge([state] + [jnp.roll(fetch(state, name, d), d, dim) for d in range(1, AXES[name][2])])
    row_top, row_total, moment, picked = state.reshape(4, -1)
    token_loss = jnp.log(row_total) + row_top - picked
    inner = moment / row_total + (row_top - picked)
    probable = jnp.exp(logits - row_top[:, None]) / row_total[:, None]
    logit_grad = (probable - target_hit.astype(F32)).astype(BF16)
    return token_loss, logit_grad, inner


def body(hidden_rows, join_weight, norm_gain, head_weight, targets):
    tok_index = lax.axis_index("tok")
    voc_index = lax.axis_index("vocab")
    width = join_weight.shape[1]
    full_width = width * 8
    rep = hidden_rows.shape[0]
    depth = join_weight.shape[0]
    own = targets.shape[0] // 8

    def relative(value):
        value = to_relative(to_relative(to_relative(value, 0, "zh"), 1, "x"), 2, "c")
        return value.transpose((2, 1, 0) + tuple(range(3, value.ndim)))

    wanted = lax.dynamic_slice_in_dim(targets, tok_index * own, own, 0)
    wanted = relative(wanted.reshape(2, 4, 2, rep)).reshape(-1)

    spread = lax.all_to_all(hidden_rows, "vocab", split_axis=1, concat_axis=0, tiled=True)
    spread = relative(spread.reshape(2, 4, 2, rep, depth))
    rows = 8 * rep
    inputs = jnp.concatenate(gather_tok(spread.reshape(16, rep, depth), 6, False), 0)
    inputs = inputs.reshape(2, 4, 2, rows, depth)

    joined = sum_vocab(inputs[0], inputs[1], join_weight, (((1,), (0,)), ((), ())), 8.0, True)
    squares = sum_tok_rows(jnp.sum(joined * joined, axis=1).reshape(2, 4, rep)).reshape(-1)
    inverse_rms = lax.rsqrt(squares / full_width + epsilon)[:, None]
    unit_rows = joined * inverse_rms
    normed = gather_vocab((unit_rows * norm_gain).astype(BF16))
    near, far = (part.reshape(4, 2, 2, 4, rep, width) for part in normed)
    logits = sum_tok(near, far, head_weight, 1.0 / 16)
    token_loss, logit_grad, inner = softmax_rows(logits, wanted, voc_index * head_weight.shape[1], rep)
    token_loss = token_loss.reshape(2, 4, 2, rep).transpose(2, 1, 0, 3)
    token_loss = to_absolute(to_absolute(to_absolute(token_loss, 0, "zh"), 1, "x"), 2, "c").reshape(-1)
    inner = gather_slots(gather_slots(inner[:rep], "y"), "z").reshape(-1, 1)

    left = jnp.pad(inputs, ((0, 0), (0, 0), (0, 0), (0, 8), (0, 0))).reshape(-1, depth)
    grads = [part.reshape(4, 2, rows, -1) for part in gather_tok(logit_grad.reshape(16, rep, -1), 8, True)]
    grads[1], left = lax.optimization_barrier((grads[1], left))
    dnormed = sum_vocab(grads[0], grads[1], head_weight, (((1,), (1,)), ((), ())), 1024.0, False)
    unit_grad = dnormed * norm_gain
    dfused = (inverse_rms * (unit_grad - unit_rows * (inner / full_width))).astype(BF16)

    gain = jnp.sum(dnormed * unit_rows, axis=0)
    pieces = []
    for _ in range(3):
        piece = lax.reduce_precision(gain, 8, 7)
        gain = gain - piece
        pieces.append(piece.astype(BF16))
    extra = jnp.stack(pieces + [jnp.zeros_like(pieces[0])] * 5)
    message = jnp.stack(gather_vocab(jnp.concatenate([dfused, extra], 0)))
    gain_grad = jnp.sum(message[:, :, :, rows : rows + 3].astype(F32), axis=(0, 1, 2, 3))
    join_grad = lax.dot_general(
        left, message.reshape(-1, width), (((0,), (0,)), ((), ())), preferred_element_type=F32
    )
    return (token_loss, gain_grad, join_grad.astype(BF16))


def solution(mesh):
    placed = (P(("tok", "vocab"), None), P("vocab", "tok"), P("tok"), P("tok", "vocab"), P())
    return jax.shard_map(
        body,
        mesh=mesh,
        in_specs=placed,
        out_specs=(P("tok"), P("tok"), P("vocab", "tok")),
        check_vma=False,
    )
```
